256 devices in a mesh: dp: 32 (over z_lo, y, core), tensor: 8 (over z_hi, x).
Axes of the slice: x: 4, y: 4, z: 8 (z_hi: 2, z_lo: 4; z = z_hi * 4 + z_lo), core: 2. Of those that a mesh axis runs over, the one named last changes fastest.
Arguments:
- tokens: bfloat16 [512, 8192], P('dp', 'tensor'), may hold values from -6 to 6
- reflectors: float32 [8192, 256], P('tensor'), may hold values from -0.0625 to 0.0625
- gate_weight: bfloat16 [8192, 28672], P('tensor', 'dp'), may hold values from -0.0625 to 0.0625
- up_weight: bfloat16 [8192, 28672], P('tensor', 'dp'), may hold values from -0.0625 to 0.0625
- down_weight: bfloat16 [28672, 8192], P('dp', 'tensor'), may hold values from -0.03125 to 0.03125
- grad_out: bfloat16 [512, 8192], P('dp', 'tensor'), may hold values from -0.059814453 to 0.059814453
Outputs:
- mixed: bfloat16 [512, 8192], P('dp', 'tensor')
- reflector_grad: float32 [8192, 256], P('tensor')
The draws below stay inside these ranges and needn't reach their ends.
All inputs are finite; a program needn't handle non-finite values.
Results may differ from the reference program's by a relative error of at most 0.0065.
Values may be sent and summed in bfloat16 or wider, within the bound.
A program may use at most 128 MiB of HBM per device.

```python
import jax
import jax.numpy as jnp
from jax import lax

D = 8192
FF = 28672
R = 256
TOKENS = 512


def level_of(key, shape, shards, low, high):
    level, own = 1.0, jax.random.fold_in(key, 6)
    for axis_at, blocks in shards:
        draws = jnp.exp(jax.random.uniform(jax.random.fold_in(own, axis_at), (blocks,), jnp.float32, low / len(shards), high / len(shards)))
        level = level * jnp.repeat(draws, shape[axis_at] // blocks).reshape([-1 if axis == axis_at else 1 for axis in range(len(shape))])
    return level


def centred(stream_key, dims, spread, limit, pieces=(), dtype=jnp.bfloat16):
    drawn = jax.random.normal(stream_key, dims, jnp.float32) * spread
    if len(pieces) > 0:
        drawn = level_of(stream_key, dims, pieces, -0.22, 0.18) * drawn
    return jnp.clip(drawn, min=-limit, max=limit).astype(dtype)


def setup_inputs(seed: int = 0) -> dict:
    key_list = jax.random.split(jax.random.key(seed), 7)
    return {
        "tokens": centred(key_list[0], (TOKENS, D), 1.0, 6.0, ((0, 32), (1, 8))),
        "reflectors": centred(key_list[1], (D, R), D ** -0.5, 0.0625, ((0, 8),), jnp.float32),
        "gate_weight": centred(key_list[2], (D, FF), D ** -0.5, 0.0625, ((0, 8), (1, 32))),
        "up_weight": centred(key_list[3], (D, FF), D ** -0.5, 0.0625, ((0, 8), (1, 32))),
        "down_weight": centred(key_list[4], (FF, D), FF ** -0.5, 0.03125, ((0, 32), (1, 8))),
        "grad_out": centred(key_list[5], (TOKENS, D), 0.01, 0.059814453, ((0, 32), (1, 8))),
    }


def reference(tokens, reflectors, gate_weight, up_weight, down_weight, grad_out):
    highest = lax.Precision.HIGHEST
    acts = tokens.astype(jnp.float32)
    gram = jnp.dot(reflectors.T, reflectors, precision=highest)
    coupling = jnp.triu(gram, 1) + 0.5 * jnp.diag(jnp.diag(gram))
    proj = jnp.dot(acts, reflectors, precision=highest)
    coeffs = jax.scipy.linalg.solve_triangular(coupling, proj.T, trans='T', lower=False).T
    reflected = (acts - jnp.dot(coeffs, reflectors.T, precision=highest)).astype(jnp.bfloat16)
    gate = jnp.dot(reflected.astype(jnp.float32), gate_weight.astype(jnp.float32), preferred_element_type=jnp.float32)
    up = jnp.dot(reflected.astype(jnp.float32), up_weight.astype(jnp.float32), preferred_element_type=jnp.float32)
    sigma = jax.nn.sigmoid(gate)
    hidden = (gate * sigma * up).astype(jnp.bfloat16)
    mixed = jnp.dot(hidden.astype(jnp.float32), down_weight.astype(jnp.float32), preferred_element_type=jnp.float32).astype(jnp.bfloat16)
    d_hidden = jnp.dot(grad_out.astype(jnp.float32), down_weight.T.astype(jnp.float32), preferred_element_type=jnp.float32)
    d_gate = (d_hidden * up * sigma * (1.0 + gate * (1.0 - sigma))).astype(jnp.bfloat16)
    d_up = (d_hidden * gate * sigma).astype(jnp.bfloat16)
    d_reflected = jnp.dot(d_gate.astype(jnp.float32), gate_weight.T.astype(jnp.float32), preferred_element_type=jnp.float32)
    d_reflected = d_reflected + jnp.dot(d_up.astype(jnp.float32), up_weight.T.astype(jnp.float32), preferred_element_type=jnp.float32)
    d_coeffs = -jnp.dot(d_reflected, reflectors, precision=highest)
    d_proj = jax.scipy.linalg.solve_triangular(coupling, d_coeffs.T, lower=False).T
    cross = jnp.dot(coeffs.T, d_proj, precision=highest)
    d_coupling = -cross
    d_gram = jnp.triu(d_coupling, 1) + 0.5 * jnp.diag(jnp.diag(d_coupling))
    grad = -jnp.dot(d_reflected.T, coeffs, precision=highest) + jnp.dot(acts.T, d_proj, precision=highest)
    grad = grad + jnp.dot(reflectors, d_gram + d_gram.T, precision=highest)
    return (mixed, grad)
```

```python
import functools

import jax
import jax.numpy as jnp
from jax import lax
from jax.experimental import pallas as pl
from jax.experimental.pallas import tpu as pltpu
from jax.sharding import PartitionSpec as P

MESH = pl.DeviceIdType.MESH
BF = jnp.bfloat16
F32 = jnp.float32
HI = lax.Precision.HIGHEST

D, FF, R, TOKENS = 8192, 28672, 256, 512
DB = D // 8
FB = FF // 32
TB = TOKENS // 32
GB = R // 32
DO = DB // 32
SEMS = 144


def nn(a, b):
    return jnp.dot(a, b, preferred_element_type=F32)


def nt(a, b):
    return lax.dot_general(a, b, (((1,), (1,)), ((), ())), preferred_element_type=F32)


def split(v):
    high = v.astype(BF)
    return high, (v - high.astype(F32)).astype(BF)


def kernel(
    tok_ref, refl_ref, gate_hbm, up_hbm, down_hbm, gout_ref, mixed_ref, grad_ref,
    gate_v, up_v, down_v, tok_all, gout_all, tok_t, refl_t, gram_v, inv_v,
    gp_send, gp_xr, gp_zs, gp_zr, gp_all,
    rg_hi, rg_lo, base_v, coef_hi, coef_lo, coef_t,
    p_send, p_xr, p_own, p_zs, p_zr, pre_v,
    h_all,
    mx_cs, mx_cr, mx_own, mx_ys, mx_yr, mx_zs, mx_zr,
    dc_cs, dc_cr, dc_own, dc_ys, dc_yr, dc_zs, dc_zr, dc_xs, dc_xr, dc_hs, dc_hr, dp_all,
    g_cs, g_cr, g_own, g_ys, g_yr, g_zs, g_zr, g_all,
    load_sem, send_sem, recv_sem,
):
    dp = lax.axis_index("dp")
    ten = lax.axis_index("tensor")
    core = lax.rem(dp, 2)
    y = lax.rem(dp // 2, 4)
    zl = dp // 8
    x = lax.rem(ten, 4)
    zh = ten // 4

    def to_x(i):
        return (dp, zh * 4 + lax.rem(x + i, 4))

    def to_zh():
        return (dp, (1 - zh) * 4 + x)

    def to_y(i):
        return ((zl * 4 + lax.rem(y + i, 4)) * 2 + core, ten)

    def to_zl(i):
        return ((lax.rem(zl + i, 4) * 4 + y) * 2 + core, ten)

    def to_core():
        return ((zl * 4 + y) * 2 + 1 - core, ten)

    peers = [to_x(1), to_x(2), to_x(3), to_zh(), to_y(1), to_y(2), to_y(3)]
    peers += [to_zl(1), to_zl(2), to_zl(3), to_core()]

    copies = []

    def send(src, dst, device):
        at = len(copies)
        copy = pltpu.make_async_remote_copy(
            src_ref=src,
            dst_ref=dst,
            send_sem=send_sem.at[at],
            recv_sem=recv_sem.at[at],
            device_id=device,
            device_id_type=MESH,
        )
        copy.start()
        copies.append(copy)
        return copy

    def land(batch):
        for copy in batch:
            copy.wait_recv()

    def rows_own(n):
        return pl.ds(pl.multiple_of((core * 16 + y * 4 + zl) * n, n), n)

    def rows_y(n):
        return pl.ds(pl.multiple_of((core * 16 + y * 4) * n, 4 * n), 4 * n)

    def rows_core(n):
        return pl.ds(pl.multiple_of(core * 16 * n, 16 * n), 16 * n)

    def gather_zl(buf, n):
        return [send(buf.at[rows_own(n)], buf.at[rows_own(n)], to_zl(i)) for i in (1, 2, 3)]

    def gather_y(buf, n):
        return [send(buf.at[rows_y(n)], buf.at[rows_y(n)], to_y(i)) for i in (1, 2, 3)]

    def gather_core(buf, n):
        return [send(buf.at[rows_core(n)], buf.at[rows_core(n)], to_core())]

    loads = [
        pltpu.make_async_copy(src, dst, load_sem.at[i])
        for i, (src, dst) in enumerate(((down_hbm, down_v), (gate_hbm, gate_v), (up_hbm, up_v)))
    ]
    for load in loads:
        load.start()

    barrier = pltpu.get_barrier_semaphore()
    for peer in peers:
        pl.semaphore_signal(barrier, inc=1, device_id=peer, device_id_type=MESH)
    tok_all[rows_own(TB), :] = tok_ref[...]
    gout_all[rows_own(TB), :] = gout_ref[...]
    pl.semaphore_wait(barrier, len(peers))

    gout_zl = gather_zl(gout_all, TB)
    tok_zl = gather_zl(tok_all, TB)

    proj = jnp.dot(tok_ref[...].astype(F32), refl_ref[...], precision=HI, preferred_element_type=F32)
    gp_send[0:TB, :] = proj
    refl_t[...] = jnp.transpose(refl_ref[...])
    gram_v[...] = jnp.dot(refl_t[...], refl_ref[...], precision=HI, preferred_element_type=F32)
    gp_send[TB:, :] = gram_v[rows_own(GB), :]
    gp_x = [send(gp_send, gp_xr.at[i - 1], to_x(i)) for i in (1, 2, 3)]

    land(gout_zl)
    gout_y = gather_y(gout_all, TB)
    land(tok_zl)
    tok_y = gather_y(tok_all, TB)

    land(gp_x)
    gp_zs[...] = gp_send[...] + gp_xr[0] + gp_xr[1] + gp_xr[2]
    gp_z = send(gp_zs, gp_zr, to_zh())

    land(gout_y)
    gout_core = gather_core(gout_all, TB)

    weights = (gate_v, up_v)
    loads[1].wait()
    loads[2].wait()
    t_hi, t_lo = split(refl_t[...])
    for u in range(2):
        rg = nn(t_hi, weights[u][...]) + nn(t_lo, weights[u][...])
        hi, lo = split(rg)
        rg_hi[u] = hi
        rg_lo[u] = lo

    gp_z.wait_recv()
    own_q = core * 16 + y * 4 + zl
    gp_all[own_q] = gp_zs[...] + gp_zr[...]
    gp_zl = gather_zl(gp_all, 1)

    loads[0].wait()
    land(gout_core)

    def x_rows(i):
        return pl.ds(pl.multiple_of(lax.rem(x + i, 4) * 128, 128), 128)

    def reduce_x(u, block):
        started = []
        for i in (2, 1, 3):
            p_send[u, x_rows(i), :] = block(x_rows(i)).astype(BF)
            started.append(send(p_send.at[u, x_rows(i)], p_xr.at[u, i - 1], to_x(i)))
        p_own[u] = block(x_rows(0))
        return started

    def reduce_zh(u, started):
        land(started)
        total = p_own.at[u]
        total[...] = (
            total[...] + p_xr[u, 0].astype(F32) + p_xr[u, 1].astype(F32) + p_xr[u, 2].astype(F32)
        )
        other = pl.ds(pl.multiple_of((1 - zh) * 64, 64), 64)
        p_zs[u] = p_own[u, other, :].astype(BF)
        return send(p_zs.at[u], p_zr.at[u], to_zh())

    def reduced(u, started):
        started.wait_recv()
        mine = pl.ds(pl.multiple_of(zh * 64, 64), 64)
        return p_own[u, mine, :] + p_zr[u].astype(F32)

    dh_x = reduce_x(2, lambda rows: nt(gout_all[rows, :], down_v[...]))

    land(gp_zl)
    gp_y = gather_y(gp_all, 1)
    land(tok_y)
    tok_core = gather_core(tok_all, TB)

    land(tok_core)
    for u in range(2):
        w = weights[u]

        def product(i, carry, u=u, w=w):
            rows = pl.ds(pl.multiple_of(i * 256, 256), 256)
            base_v[u, rows, :] = nn(tok_all[rows, :], w[...])
            return carry

        lax.fori_loop(0, 2, product, 0)

    land(gp_y)
    gp_core = gather_core(gp_all, 1)
    dh_z = reduce_zh(2, dh_x)
    land(gp_core)

    gram = gp_all[:, TB:, :].reshape(R, R)
    row = lax.broadcasted_iota(jnp.int32, (R, R), 0)
    col = lax.broadcasted_iota(jnp.int32, (R, R), 1)
    eye = row == col
    diag_col = 0.5 * jnp.sum(jnp.where(eye, gram, 0.0), axis=1, keepdims=True)
    diag_row = 0.5 * jnp.sum(jnp.where(eye, gram, 0.0), axis=0, keepdims=True)
    gram_v[...] = jnp.where(col > row, gram, 0.0) / diag_col
    first = (col == row + 1) & ((row & 1) == 0)
    inv_v[...] = jnp.where(eye, 1.0, 0.0) - jnp.where(first, gram_v[...], 0.0)

    def double(level, carry):
        rb = lax.shift_right_logical(row, level)
        cb = lax.shift_right_logical(col, level)
        corner = (cb == rb + 1) & ((rb & 1) == 0)
        m = jnp.where(corner, gram_v[...], 0.0)
        half = jnp.dot(m, inv_v[...], precision=HI, preferred_element_type=F32)
        inv_v[...] -= jnp.dot(inv_v[...], half, precision=HI, preferred_element_type=F32)
        return carry

    lax.fori_loop(1, 8, double, 0)
    inv_v[...] = inv_v[...] / diag_row

    proj_all = gp_all[:, :TB, :].reshape(TOKENS, R)
    coeffs = jnp.dot(proj_all, inv_v[...], precision=HI, preferred_element_type=F32)
    hi, lo = split(coeffs)
    coef_hi[...] = hi
    coef_lo[...] = lo

    def pre_block(u):
        def block(rows):
            ch = coef_hi[rows, :]
            moved = nn(ch, rg_hi[u]) + nn(ch, rg_lo[u]) + nn(coef_lo[rows, :], rg_hi[u])
            return base_v[u, rows, :] - moved

        return block

    gate_x = reduce_x(0, pre_block(0))
    up_x = reduce_x(1, pre_block(1))

    coef_t[...] = jnp.transpose(coeffs)
    tok_t[...] = jnp.transpose(tok_all[...])
    d_hidden = reduced(2, dh_z)
    pre_v[2] = d_hidden

    gate_z = reduce_zh(0, gate_x)
    up_z = reduce_zh(1, up_x)
    pre_v[0] = reduced(0, gate_z)
    pre_v[1] = reduced(1, up_z)

    gate = pre_v[0]
    up = pre_v[1]
    d_hidden = pre_v[2]
    sigma = jax.nn.sigmoid(gate)
    share = pl.ds(pl.multiple_of(x * 128 + zh * 64, 64), 64)
    other = pl.ds(pl.multiple_of(x * 128 + (1 - zh) * 64, 64), 64)
    h_all[0, share, :] = (d_hidden * up * sigma * (1.0 + gate * (1.0 - sigma))).astype(BF)
    h_all[1, share, :] = (d_hidden * gate * sigma).astype(BF)
    h_all[2, share, :] = (gate * sigma * up).astype(BF)

    h_z, h_x, h_x2 = [], [], []
    for u in range(3):
        h_z.append(send(h_all.at[u, share], h_all.at[u, share], to_zh()))
        h_x.append([send(h_all.at[u, share], h_all.at[u, share], to_x(i)) for i in (2, 1, 3)])
    for u in range(3):
        h_z[u].wait_recv()
        h_x2.append([send(h_all.at[u, other], h_all.at[u, other], to_x(i)) for i in (2, 1, 3)])

    def land_unit(u):
        land(h_x[u])
        land(h_x2[u])

    half_own = pl.ds(pl.multiple_of(core * 256, 256), 256)
    half_other = pl.ds(pl.multiple_of((1 - core) * 256, 256), 256)

    land_unit(0)
    land_unit(1)

    def dc_block(rows):
        total = nt(h_all[0, rows, :], rg_hi[0]) + nt(h_all[0, rows, :], rg_lo[0])
        return total + nt(h_all[1, rows, :], rg_hi[1]) + nt(h_all[1, rows, :], rg_lo[1])

    def scatter_y(own, sent, got, n, dtype):
        started = []
        for i in (2, 1, 3):
            rows = pl.ds(pl.multiple_of(lax.rem(y + i, 4) * 4 * n, 4 * n), 4 * n)
            sent[i - 1] = own[rows, :].astype(dtype)
            started.append(send(sent.at[i - 1], got.at[i - 1], to_y(i)))
        return started

    def after_y(own, got, started, n):
        land(started)
        rows = pl.ds(pl.multiple_of(y * 4 * n, 4 * n), 4 * n)
        own[rows, :] = own[rows, :] + got[0].astype(F32) + got[1].astype(F32) + got[2].astype(F32)

    def scatter_zl(own, sent, got, n, dtype):
        started = []
        for i in (2, 1, 3):
            rows = pl.ds(pl.multiple_of((y * 4 + lax.rem(zl + i, 4)) * n, n), n)
            sent[i - 1] = own[rows, :].astype(dtype)
            started.append(send(sent.at[i - 1], got.at[i - 1], to_zl(i)))
        return started

    def after_zl(own, got, started, n):
        land(started)
        rows = pl.ds(pl.multiple_of((y * 4 + zl) * n, n), n)
        return own[rows, :] + got[0].astype(F32) + got[1].astype(F32) + got[2].astype(F32)

    dc_cs[...] = dc_block(half_other)
    dc_c = send(dc_cs, dc_cr, to_core())
    dc_own[...] = dc_block(half_own)
    dc_c.wait_recv()
    dc_own[...] = dc_own[...] + dc_cr[...]
    dc_y = scatter_y(dc_own, dc_ys, dc_yr, TB, F32)

    t_hi, t_lo = split(coef_t[...])
    q0_hi, q0_lo = split(nn(t_hi, h_all[0]) + nn(t_lo, h_all[0]))
    q1_hi, q1_lo = split(nn(t_hi, h_all[1]) + nn(t_lo, h_all[1]))

    def g_block(rows):
        total = nt(gate_v[rows, :], q0_hi) + nt(gate_v[rows, :], q0_lo)
        return -(total + nt(up_v[rows, :], q1_hi) + nt(up_v[rows, :], q1_lo))

    g_half_own = pl.ds(pl.multiple_of(core * 512, 512), 512)
    g_half_other = pl.ds(pl.multiple_of((1 - core) * 512, 512), 512)
    g_cs[...] = g_block(g_half_other).astype(BF)
    g_c = send(g_cs, g_cr, to_core())

    after_y(dc_own, dc_yr, dc_y, TB)
    dc_z = scatter_zl(dc_own, dc_zs, dc_zr, TB, F32)

    g_own[...] = g_block(g_half_own)
    g_c.wait_recv()
    g_own[...] = g_own[...] + g_cr[...].astype(F32)
    g_y = scatter_y(g_own, g_ys, g_yr, DO, BF)

    dc_xs[...] = after_zl(dc_own, dc_zr, dc_z, TB)
    dc_x = [send(dc_xs, dc_xr.at[i - 1], to_x(i)) for i in (1, 2, 3)]

    land_unit(2)
    mx_cs[...] = nn(h_all[2, half_other, :], down_v[...]).astype(BF)
    mx_c = send(mx_cs, mx_cr, to_core())

    land(dc_x)
    dc_hs[...] = dc_xs[...] + dc_xr[0] + dc_xr[1] + dc_xr[2]
    dc_h = send(dc_hs, dc_hr, to_zh())

    after_y(g_own, g_yr, g_y, DO)
    g_z = scatter_zl(g_own, g_zs, g_zr, DO, BF)

    mx_own[...] = nn(h_all[2, half_own, :], down_v[...])
    mx_c.wait_recv()
    mx_own[...] = mx_own[...] + mx_cr[...].astype(F32)
    mx_y = scatter_y(mx_own, mx_ys, mx_yr, TB, BF)

    dc_h.wait_recv()
    d_coeffs = -(dc_hs[...] + dc_hr[...])
    dp_all[rows_own(TB), :] = lax.dot_general(
        d_coeffs, inv_v[...], (((1,), (1,)), ((), ())), precision=HI, preferred_element_type=F32
    )
    dp_zl = gather_zl(dp_all, TB)

    g_all[rows_own(DO), :] = after_zl(g_own, g_zr, g_z, DO).astype(BF)
    g_zl = gather_zl(g_all, DO)

    land(dp_zl)
    dp_y = gather_y(dp_all, TB)

    after_y(mx_own, mx_yr, mx_y, TB)
    mx_z = scatter_zl(mx_own, mx_zs, mx_zr, TB, BF)

    land(g_zl)
    g_y2 = gather_y(g_all, DO)

    land(dp_y)
    dp_core = gather_core(dp_all, TB)
    mixed_ref[...] = after_zl(mx_own, mx_zr, mx_z, TB).astype(BF)
    land(dp_core)

    d_coupling = -jnp.dot(coef_t[...], dp_all[...], precision=HI, preferred_element_type=F32)
    sym = jnp.where(col >= row, d_coupling, jnp.transpose(d_coupling))
    d_hi, d_lo = split(dp_all[...])
    land(g_y2)
    g_core = gather_core(g_all, DO)
    total = nn(tok_t[...], d_hi) + nn(tok_t[...], d_lo)
    total = total + jnp.dot(refl_ref[...], sym, precision=HI, preferred_element_type=F32)
    land(g_core)
    grad_ref[...] = total + g_all[...].astype(F32)

    for copy in copies:
        copy.wait_send()


def scratch():
    v = pltpu.VMEM
    dma = pltpu.SemaphoreType.DMA
    own = TB + GB
    return [
        v((DB, FB), BF), v((DB, FB), BF), v((FB, DB), BF),
        v((TOKENS, DB), BF), v((TOKENS, DB), BF), v((DB, TOKENS), BF), v((R, DB), F32), v((R, R), F32), v((R, R), F32),
        v((own, R), F32), v((3, own, R), F32), v((own, R), F32), v((own, R), F32), v((32, own, R), F32),
        v((2, R, FB), BF), v((2, R, FB), BF), v((2, TOKENS, FB), F32),
        v((TOKENS, R), BF), v((TOKENS, R), BF), v((R, TOKENS), F32),
        v((3, TOKENS, FB), BF), v((3, 3, 128, FB), BF), v((3, 128, FB), F32),
        v((3, 64, FB), BF), v((3, 64, FB), BF), v((3, 64, FB), F32),
        v((3, TOKENS, FB), BF),
        v((256, DB), BF), v((256, DB), BF), v((256, DB), F32),
        v((3, 64, DB), BF), v((3, 64, DB), BF), v((3, TB, DB), BF), v((3, TB, DB), BF),
        v((256, R), F32), v((256, R), F32), v((256, R), F32),
        v((3, 64, R), F32), v((3, 64, R), F32), v((3, TB, R), F32), v((3, TB, R), F32),
        v((TB, R), F32), v((3, TB, R), F32), v((TB, R), F32), v((TB, R), F32), v((TOKENS, R), F32),
        v((512, R), BF), v((512, R), BF), v((512, R), F32),
        v((3, 4 * DO, R), BF), v((3, 4 * DO, R), BF), v((3, DO, R), BF), v((3, DO, R), BF), v((DB, R), BF),
        dma((3,)), dma((SEMS,)), dma((SEMS,)),
    ]


def body(tokens, reflectors, gate_weight, up_weight, down_weight, grad_out):
    whole = pl.BlockSpec(memory_space=pltpu.VMEM)
    far = pl.BlockSpec(memory_space=pl.ANY)
    return pl.pallas_call(
        kernel,
        out_shape=(
            jax.ShapeDtypeStruct((TB, DB), BF),
            jax.ShapeDtypeStruct((DB, R), F32),
        ),
        in_specs=[whole, whole, far, far, far, whole],
        out_specs=(whole, whole),
        scratch_shapes=scratch(),
        compiler_params=pltpu.CompilerParams(
            collective_id=0, has_side_effects=True, vmem_limit_bytes=56 << 20
        ),
    )(tokens, reflectors, gate_weight, up_weight, down_weight, grad_out)


def solution(mesh):
    placed = (
        P("dp", "tensor"),
        P("tensor", None),
        P("tensor", "dp"),
        P("tensor", "dp"),
        P("dp", "tensor"),
        P("dp", "tensor"),
    )
    return jax.shard_map(
        body,
        mesh=mesh,
        in_specs=placed,
        out_specs=(P("dp", "tensor"), P("tensor", None)),
        check_vma=False,
    )
```

```python
import functools

import jax
import jax.numpy as jnp
from jax import lax
from jax.experimental import pallas as pl
from jax.experimental.pallas import tpu as pltpu
from jax.sharding import PartitionSpec as P

MESH = pl.DeviceIdType.MESH
BF = jnp.bfloat16
F32 = jnp.float32
HI = lax.Precision.HIGHEST

D, FF, R, TOKENS = 8192, 28672, 256, 512
DB = D // 8
FB = FF // 32
TB = TOKENS // 32
DO = DB // 32
SEMS = 224
ALL_COLS = pl.ds(0, FB)
HALVES = (pl.ds(0, 512), pl.ds(512, 384))
COLS = (pl.ds(0, 128), pl.ds(128, 256), pl.ds(384, 256), pl.ds(640, 256))


def nn(a, b):
    return jnp.dot(a, b, preferred_element_type=F32)


def nt(a, b):
    return lax.dot_general(a, b, (((1,), (1,)), ((), ())), preferred_element_type=F32)


def split(v):
    high = v.astype(BF)
    return high, (v - high.astype(F32)).astype(BF)


def kernel(
    tok_hbm, refl_hbm, gate_hbm, up_hbm, down_hbm, gout_hbm, mixed_ref, grad_ref,
    refl_v, gate_v, up_v, down_v, tok_all, gout_all, tok_t, refl_t, gram_v, unit_v, inv_v,
    gram_all, gm_xr, gm_zs, gm_zr, pj_send, pj_xr, pj_zs, pj_zr, pj_all,
    rg_hi, rg_lo, reflected, coef_v, coef_t,
    p_send, p_xr, p_own, p_zs, p_zr,
    h_all,
    mx_cs, mx_cr, mx_own, mx_ys, mx_yr, mx_zs, mx_zr,
    dc_cs, dc_cr, dc_own, dc_ys, dc_yr, dc_zs, dc_zr, dc_xs, dc_xr, dc_hs, dc_hr, dp_all,
    g_cs, g_cr, g_own, g_ys, g_yr, g_zs, g_zr, g_all,
    load_sem, send_sem, recv_sem,
):
    dp = lax.axis_index("dp")
    ten = lax.axis_index("tensor")
    core = lax.rem(dp, 2)
    y = lax.rem(dp // 2, 4)
    zl = dp // 8
    x = lax.rem(ten, 4)
    zh = ten // 4

    def to_x(i):
        return (dp, zh * 4 + lax.rem(x + i, 4))

    def to_zh():
        return (dp, (1 - zh) * 4 + x)

    def to_y(i):
        return ((zl * 4 + lax.rem(y + i, 4)) * 2 + core, ten)

    def to_zl(i):
        return ((lax.rem(zl + i, 4) * 4 + y) * 2 + core, ten)

    def to_core():
        return ((zl * 4 + y) * 2 + 1 - core, ten)

    peers = [to_x(1), to_x(2), to_x(3), to_zh(), to_y(1), to_y(2), to_y(3)]
    peers += [to_zl(1), to_zl(2), to_zl(3), to_core()]

    copies = []

    def send(src, dst, device):
        at = len(copies)
        copy = pltpu.make_async_remote_copy(
            src_ref=src,
            dst_ref=dst,
            send_sem=send_sem.at[at],
            recv_sem=recv_sem.at[at],
            device_id=device,
            device_id_type=MESH,
        )
        copy.start()
        copies.append(copy)
        return copy

    def land(batch):
        for copy in batch:
            copy.wait_recv()

    def rows_own(n):
        return pl.ds(pl.multiple_of((core * 16 + y * 4 + zl) * n, n), n)

    def rows_y(n):
        return pl.ds(pl.multiple_of((core * 16 + y * 4) * n, 4 * n), 4 * n)

    def rows_core(n):
        return pl.ds(pl.multiple_of(core * 16 * n, 16 * n), 16 * n)

    def gather_zl(buf, n):
        return [send(buf.at[rows_own(n)], buf.at[rows_own(n)], to_zl(i)) for i in (1, 2, 3)]

    def gather_y(buf, n):
        return [send(buf.at[rows_y(n)], buf.at[rows_y(n)], to_y(i)) for i in (1, 2, 3)]

    def gather_core(buf, n):
        return [send(buf.at[rows_core(n)], buf.at[rows_core(n)], to_core())]

    def gather_start(buf, n):
        own = buf.at[rows_own(n)]
        along_zl = [send(own, own, to_zl(i)) for i in (1, 2, 3)]
        return along_zl, [send(own, own, to_y(i)) for i in (1, 2, 3)]

    def gather_rest(buf, n, started):
        along_zl, along_y = started
        for i, copy in zip((1, 2, 3), along_zl):
            copy.wait_recv()
            at = core * 16 + y * 4 + lax.rem(zl + 4 - i, 4)
            came = buf.at[pl.ds(pl.multiple_of(at * n, n), n)]
            along_y.extend(send(came, came, to_y(k)) for k in (1, 2, 3))
        return along_y

    loads = [
        pltpu.make_async_copy(src, dst, load_sem.at[i])
        for i, (src, dst) in enumerate(
            (
                (refl_hbm, refl_v),
                (tok_hbm, tok_all.at[rows_own(TB)]),
                (gout_hbm, gout_all.at[rows_own(TB)]),
                (gate_hbm, gate_v),
                (up_hbm, up_v),
                (down_hbm, down_v),
            )
        )
    ]
    for load in loads:
        load.start()

    barrier = pltpu.get_barrier_semaphore()
    for peer in peers:
        pl.semaphore_signal(barrier, inc=1, device_id=peer, device_id_type=MESH)

    loads[2].wait()
    pl.semaphore_wait(barrier, len(peers))
    gout_start = gather_start(gout_all, TB)

    loads[0].wait()
    my_half = pl.ds(pl.multiple_of(core * 128, 128), 128)
    columns = jnp.transpose(refl_v[:, my_half])
    gram_v[my_half, :] = jnp.dot(columns, refl_v[...], precision=HI, preferred_element_type=F32)

    def gram_rows(i):
        return pl.ds(pl.multiple_of(core * 128 + lax.rem(x + i, 4) * 32, 32), 32)

    gram_x = [send(gram_v.at[gram_rows(i)], gm_xr.at[i - 1], to_x(i)) for i in (2, 1, 3)]
    gout_y = gather_rest(gout_all, TB, gout_start)
    loads[1].wait()
    own_tok = tok_all[rows_own(TB), :].astype(F32)
    pj_send[...] = jnp.dot(own_tok, refl_v[...], precision=HI, preferred_element_type=F32)
    pj_x = [send(pj_send, pj_xr.at[i - 1], to_x(i)) for i in (2, 1, 3)]
    tok_zl = gather_zl(tok_all, TB)

    land(gram_x)
    gm_zs[...] = gram_v[gram_rows(0), :] + gm_xr[0] + gm_xr[1] + gm_xr[2]
    gram_z = send(gm_zs, gm_zr, to_zh())
    land(pj_x)
    pj_zs[...] = pj_send[...] + pj_xr[0] + pj_xr[1] + pj_xr[2]
    pj_z = send(pj_zs, pj_zr, to_zh())

    land(gout_y)
    gout_core = gather_core(gout_all, TB)
    land(tok_zl)
    tok_y = gather_y(tok_all, TB)

    def x_rows(i):
        return pl.ds(pl.multiple_of(lax.rem(x + i, 4) * 128, 128), 128)

    def scatter_x(u, cols, block):
        started = []
        for i in (2, 1, 3):
            p_send[u, x_rows(i), cols] = block(x_rows(i), cols).astype(BF)
            started.append(send(p_send.at[u, x_rows(i), cols], p_xr.at[u, i - 1, :, cols], to_x(i)))
        p_own[u, :, cols] = block(x_rows(0), cols)
        return started

    def exchange_zh(u, cols, started):
        land(started)
        got = p_xr[u, 0, :, cols].astype(F32) + p_xr[u, 1, :, cols].astype(F32)
        total = p_own[u, :, cols] + got + p_xr[u, 2, :, cols].astype(F32)
        p_own[u, :, cols] = total
        p_zs[u, :, cols] = total.astype(BF)
        return send(p_zs.at[u, :, cols], p_zr.at[u, :, cols], to_zh())

    def reduced(u, cols, started):
        started.wait_recv()
        return p_own[u, :, cols] + p_zr[u, :, cols].astype(F32)

    def dh_block(rows, cols):
        return nt(gout_all[rows, :], down_v[cols, :])

    loads[5].wait()
    land(gout_core)
    dh_x = [scatter_x(2, HALVES[0], dh_block)]
    gram_z.wait_recv()
    gram_all[gram_rows(0), :] = gm_zs[...] + gm_zr[...]
    own_gram = gram_all.at[gram_rows(0)]
    gram_x = [send(own_gram, own_gram, to_x(i)) for i in (2, 1, 3)]
    pj_z.wait_recv()
    pj_all[rows_own(TB), :] = pj_zs[...] + pj_zr[...]
    pj_start = gather_start(pj_all, TB)
    dh_x.append(scatter_x(2, HALVES[1], dh_block))
    land(gram_x)
    gram_core = send(gram_all.at[my_half], gram_all.at[my_half], to_core())
    pj_y = gather_rest(pj_all, TB, pj_start)
    land(tok_y)
    tok_core = gather_core(tok_all, TB)
    gram_core.wait_recv()

    gram = gram_all[...]
    row = lax.broadcasted_iota(jnp.int32, (R, R), 0)
    col = lax.broadcasted_iota(jnp.int32, (R, R), 1)
    eye = row == col
    diag_col = 0.5 * jnp.sum(jnp.where(eye, gram, 0.0), axis=1, keepdims=True)
    diag_row = 0.5 * jnp.sum(jnp.where(eye, gram, 0.0), axis=0, keepdims=True)
    unit_v[...] = jnp.where(col > row, gram, 0.0) / diag_col
    first = (col == row + 1) & ((row & 1) == 0)
    inv_v[...] = jnp.where(eye, 1.0, 0.0) - jnp.where(first, unit_v[...], 0.0)

    def double(level, carry):
        rb = lax.shift_right_logical(row, level)
        cb = lax.shift_right_logical(col, level)
        corner = (cb == rb + 1) & ((rb & 1) == 0)
        m = jnp.where(corner, unit_v[...], 0.0)
        step = jnp.dot(m, inv_v[...], precision=HI, preferred_element_type=F32)
        inv_v[...] -= jnp.dot(inv_v[...], step, precision=HI, preferred_element_type=F32)
        return carry

    lax.fori_loop(1, 4, double, 0)
    land(pj_y)
    pj_core = gather_core(pj_all, TB)
    dh_z = [exchange_zh(2, HALVES[0], dh_x[0])]
    lax.fori_loop(4, 8, double, 0)
    inv_v[...] = inv_v[...] / diag_row
    land(pj_core)
    coef_v[...] = jnp.dot(pj_all[...], inv_v[...], precision=HI, preferred_element_type=F32)
    land(tok_core)
    r_hi, r_lo = split(refl_v[...])
    weights = (gate_v, up_v)
    loads[3].wait()
    loads[4].wait()

    def reflect(rows):
        c_hi, c_lo = split(coef_v[rows, :])
        moved = nt(c_hi, r_hi) + nt(c_lo, r_hi) + nt(c_hi, r_lo)
        reflected[rows, :] = (tok_all[rows, :].astype(F32) - moved).astype(BF)

    def pre_block(u):
        return lambda rows, cols: nn(reflected[rows, :], weights[u][:, cols])

    parts = range(len(COLS))
    pre_x, pre_z, h_x = {}, {}, {}

    def pre_scatter(j):
        for u in range(2):
            pre_x[u, j] = scatter_x(u, COLS[j], pre_block(u))

    def pre_exchange(j):
        for u in range(2):
            pre_z[u, j] = exchange_zh(u, COLS[j], pre_x[u, j])

    def give(u, cols):
        block = h_all.at[u, x_rows(0), cols]
        return [send(block, block, to_x(i)) for i in (2, 1, 3)]

    def activate(j):
        cols = COLS[j]
        gate = reduced(0, cols, pre_z[0, j])
        up = reduced(1, cols, pre_z[1, j])
        d_hidden = p_own[2, :, cols] + p_zr[2, :, cols].astype(F32)
        sigma = jax.nn.sigmoid(gate)
        h_all[0, x_rows(0), cols] = (d_hidden * up * sigma * (1.0 + gate * (1.0 - sigma))).astype(BF)
        h_all[1, x_rows(0), cols] = (d_hidden * gate * sigma).astype(BF)
        for u in range(2):
            h_x[u, j] = give(u, cols)
        h_all[2, x_rows(0), cols] = (gate * sigma * up).astype(BF)

    pre_x[0, 0], pre_x[1, 0] = [], []
    for i in (2, 1, 3, 0):
        reflect(x_rows(i))
        for u in range(2):
            value = pre_block(u)(x_rows(i), COLS[0])
            if i:
                p_send[u, x_rows(i), COLS[0]] = value.astype(BF)
                pre_x[u, 0].append(
                    send(p_send.at[u, x_rows(i), COLS[0]], p_xr.at[u, i - 1, :, COLS[0]], to_x(i))
                )
            else:
                p_own[u, :, COLS[0]] = value
    dh_z.append(exchange_zh(2, HALVES[1], dh_x[1]))
    pre_scatter(1)
    pre_exchange(0)
    pre_scatter(2)
    pre_exchange(1)
    pre_scatter(3)

    refl_t[...] = jnp.transpose(refl_v[...])
    t_hi, t_lo = split(refl_t[...])
    for u in range(2):
        rg_hi[u], rg_lo[u] = split(nn(t_hi, weights[u][...]) + nn(t_lo, weights[u][...]))
    coef_t[...] = jnp.transpose(coef_v[...])
    tok_t[...] = jnp.transpose(tok_all[...])
    land(dh_z)
    activate(0)
    pre_exchange(2)
    activate(1)
    pre_exchange(3)
    activate(2)
    activate(3)
    for j in parts:
        land(h_x[0, j] + h_x[1, j])

    hidden_x = give(2, ALL_COLS)

    half_own = pl.ds(pl.multiple_of(core * 256, 256), 256)
    half_other = pl.ds(pl.multiple_of((1 - core) * 256, 256), 256)

    def dc_block(rows):
        total = nt(h_all[0, rows, :], rg_hi[0]) + nt(h_all[0, rows, :], rg_lo[0])
        return total + nt(h_all[1, rows, :], rg_hi[1]) + nt(h_all[1, rows, :], rg_lo[1])

    def scatter_y(own, sent, got, n, dtype):
        started = []
        for i in (2, 1, 3):
            rows = pl.ds(pl.multiple_of(lax.rem(y + i, 4) * 4 * n, 4 * n), 4 * n)
            sent[i - 1] = own[rows, :].astype(dtype)
            started.append(send(sent.at[i - 1], got.at[i - 1], to_y(i)))
        return started

    def after_y(own, got, started, n):
        land(started)
        rows = pl.ds(pl.multiple_of(y * 4 * n, 4 * n), 4 * n)
        own[rows, :] = own[rows, :] + got[0].astype(F32) + got[1].astype(F32) + got[2].astype(F32)

    def scatter_zl(own, sent, got, n, dtype):
        started = []
        for i in (2, 1, 3):
            rows = pl.ds(pl.multiple_of((y * 4 + lax.rem(zl + i, 4)) * n, n), n)
            sent[i - 1] = own[rows, :].astype(dtype)
            started.append(send(sent.at[i - 1], got.at[i - 1], to_zl(i)))
        return started

    def after_zl(own, got, started, n):
        land(started)
        rows = pl.ds(pl.multiple_of((y * 4 + zl) * n, n), n)
        return own[rows, :] + got[0].astype(F32) + got[1].astype(F32) + got[2].astype(F32)

    dc_cs[...] = dc_block(half_other)
    dc_c = send(dc_cs, dc_cr, to_core())
    dc_own[...] = dc_block(half_own)
    dc_c.wait_recv()
    dc_own[...] = dc_own[...] + dc_cr[...]
    dc_y = scatter_y(dc_own, dc_ys, dc_yr, TB, F32)

    t_hi, t_lo = split(coef_t[...])
    q0_hi, q0_lo = split(nn(t_hi, h_all[0]) + nn(t_lo, h_all[0]))
    q1_hi, q1_lo = split(nn(t_hi, h_all[1]) + nn(t_lo, h_all[1]))

    def g_block(rows):
        total = nt(gate_v[rows, :], q0_hi) + nt(gate_v[rows, :], q0_lo)
        return -(total + nt(up_v[rows, :], q1_hi) + nt(up_v[rows, :], q1_lo))

    g_half_own = pl.ds(pl.multiple_of(core * 512, 512), 512)
    g_half_other = pl.ds(pl.multiple_of((1 - core) * 512, 512), 512)
    g_cs[...] = g_block(g_half_other).astype(BF)
    g_c = send(g_cs, g_cr, to_core())

    after_y(dc_own, dc_yr, dc_y, TB)
    dc_z = scatter_zl(dc_own, dc_zs, dc_zr, TB, F32)

    g_own[...] = g_block(g_half_own)
    g_c.wait_recv()
    g_own[...] = g_own[...] + g_cr[...].astype(F32)
    g_y = scatter_y(g_own, g_ys, g_yr, DO, BF)

    dc_xs[...] = after_zl(dc_own, dc_zr, dc_z, TB)
    dc_x = [send(dc_xs, dc_xr.at[i - 1], to_x(i)) for i in (1, 2, 3)]

    land(dc_x)
    dc_hs[...] = dc_xs[...] + dc_xr[0] + dc_xr[1] + dc_xr[2]
    dc_h = send(dc_hs, dc_hr, to_zh())

    land(hidden_x)
    mx_cs[...] = nn(h_all[2, half_other, :], down_v[...]).astype(BF)
    mx_c = send(mx_cs, mx_cr, to_core())

    after_y(g_own, g_yr, g_y, DO)
    g_z = scatter_zl(g_own, g_zs, g_zr, DO, BF)

    mx_own[...] = nn(h_all[2, half_own, :], down_v[...])
    mx_c.wait_recv()
    mx_own[...] = mx_own[...] + mx_cr[...].astype(F32)
    mx_y = scatter_y(mx_own, mx_ys, mx_yr, TB, BF)

    dc_h.wait_recv()
    d_coeffs = -(dc_hs[...] + dc_hr[...])
    dp_all[rows_own(TB), :] = lax.dot_general(
        d_coeffs, inv_v[...], (((1,), (1,)), ((), ())), precision=HI, preferred_element_type=F32
    )
    dp_zl = gather_zl(dp_all, TB)

    g_all[rows_own(DO), :] = after_zl(g_own, g_zr, g_z, DO).astype(BF)
    g_zl = gather_zl(g_all, DO)

    land(dp_zl)
    dp_y = gather_y(dp_all, TB)

    after_y(mx_own, mx_yr, mx_y, TB)
    mx_z = scatter_zl(mx_own, mx_zs, mx_zr, TB, BF)

    land(g_zl)
    g_y2 = gather_y(g_all, DO)

    land(dp_y)
    dp_core = gather_core(dp_all, TB)
    mixed_ref[...] = after_zl(mx_own, mx_zr, mx_z, TB).astype(BF)
    land(dp_core)

    d_coupling = -jnp.dot(coef_t[...], dp_all[...], precision=HI, preferred_element_type=F32)
    sym = jnp.where(col >= row, d_coupling, jnp.transpose(d_coupling))
    d_hi, d_lo = split(dp_all[...])
    land(g_y2)
    g_core = gather_core(g_all, DO)
    total = nn(tok_t[...], d_hi) + nn(tok_t[...], d_lo)
    total = total + jnp.dot(refl_v[...], sym, precision=HI, preferred_element_type=F32)
    land(g_core)
    grad_ref[...] = total + g_all[...].astype(F32)

    for copy in copies:
        copy.wait_send()


def scratch():
    v = pltpu.VMEM
    dma = pltpu.SemaphoreType.DMA
    return [
        v((DB, R), F32), v((DB, FB), BF), v((DB, FB), BF), v((FB, DB), BF),
        v((TOKENS, DB), BF), v((TOKENS, DB), BF), v((DB, TOKENS), BF), v((R, DB), F32), v((R, R), F32), v((R, R), F32), v((R, R), F32),
        v((R, R), F32), v((3, 32, R), F32), v((32, R), F32), v((32, R), F32),
        v((TB, R), F32), v((3, TB, R), F32), v((TB, R), F32), v((TB, R), F32), v((TOKENS, R), F32),
        v((2, R, FB), BF), v((2, R, FB), BF), v((TOKENS, DB), BF), v((TOKENS, R), F32), v((R, TOKENS), F32),
        v((3, TOKENS, FB), BF), v((3, 3, 128, FB), BF), v((3, 128, FB), F32), v((3, 128, FB), BF), v((3, 128, FB), BF),
        v((3, TOKENS, FB), BF),
        v((256, DB), BF), v((256, DB), BF), v((256, DB), F32),
        v((3, 64, DB), BF), v((3, 64, DB), BF), v((3, TB, DB), BF), v((3, TB, DB), BF),
        v((256, R), F32), v((256, R), F32), v((256, R), F32),
        v((3, 64, R), F32), v((3, 64, R), F32), v((3, TB, R), F32), v((3, TB, R), F32),
        v((TB, R), F32), v((3, TB, R), F32), v((TB, R), F32), v((TB, R), F32), v((TOKENS, R), F32),
        v((512, R), BF), v((512, R), BF), v((512, R), F32),
        v((3, 4 * DO, R), BF), v((3, 4 * DO, R), BF), v((3, DO, R), BF), v((3, DO, R), BF), v((DB, R), BF),
        dma((6,)), dma((SEMS,)), dma((SEMS,)),
    ]


def body(tokens, reflectors, gate_weight, up_weight, down_weight, grad_out):
    whole = pl.BlockSpec(memory_space=pltpu.VMEM)
    far = pl.BlockSpec(memory_space=pltpu.HBM)
    return pl.pallas_call(
        kernel,
        out_shape=(
            jax.ShapeDtypeStruct((TB, DB), BF),
            jax.ShapeDtypeStruct((DB, R), F32),
        ),
        in_specs=[far] * 6,
        out_specs=(whole, whole),
        scratch_shapes=scratch(),
        compiler_params=pltpu.CompilerParams(
            collective_id=0, has_side_effects=True, vmem_limit_bytes=52 << 20
        ),
    )(tokens, reflectors, gate_weight, up_weight, down_weight, grad_out)


def solution(mesh):
    placed = (
        P("dp", "tensor"),
        P("tensor", None),
        P("tensor", "dp"),
        P("tensor", "dp"),
        P("dp", "tensor"),
        P("dp", "tensor"),
    )
    return jax.shard_map(
        body,
        mesh=mesh,
        in_specs=placed,
        out_specs=(P("dp", "tensor"), P("tensor", None)),
        check_vma=False,
    )
```

```python
import functools

import jax
import jax.numpy as jnp
from jax import lax
from jax.experimental import pallas as pl
from jax.experimental.pallas import tpu as pltpu
from jax.sharding import PartitionSpec as P

MESH = pl.DeviceIdType.MESH
BF = jnp.bfloat16
F32 = jnp.float32
HI = lax.Precision.HIGHEST

D, FF, R, TOKENS = 8192, 28672, 256, 512
DB = D // 8
FB = FF // 32
TB = TOKENS // 32
DO = DB // 32
SEMS = 224
ALL_COLS = pl.ds(0, FB)
HALVES = (pl.ds(0, 512), pl.ds(512, 384))
COLS = (pl.ds(0, 128), pl.ds(128, 256), pl.ds(384, 256), pl.ds(640, 256))


def nn(a, b):
    return jnp.dot(a, b, preferred_element_type=F32)


def nt(a, b):
    return lax.dot_general(a, b, (((1,), (1,)), ((), ())), preferred_element_type=F32)


def split(v):
    high = v.astype(BF)
    return high, (v - high.astype(F32)).astype(BF)


def kernel(
    tok_hbm, refl_hbm, gate_hbm, up_hbm, down_hbm, gout_hbm, mixed_ref, grad_ref,
    refl_v, gate_v, up_v, down_v, tok_all, gout_all, tok_t, refl_t, gram_v, unit_v, inv_v,
    gram_all, gm_xr, gm_zs, gm_zr, pj_send, pj_xr, pj_zs, pj_zr, pj_all,
    rg_hi, rg_lo, reflected, coef_v, coef_t,
    p_send, p_xr, p_own, p_zs, p_zr,
    h_all, dc_acc, q_hi, q_lo,
    mx_cs, mx_cr, mx_own, mx_ys, mx_yr, mx_zs, mx_zr,
    dc_cs, dc_cr, dc_own, dc_ys, dc_yr, dc_zs, dc_zr, dc_xs, dc_xr, dc_hs, dc_hr, dp_all,
    g_cs, g_cr, g_own, g_ys, g_yr, g_zs, g_zr, g_all,
    load_sem, send_sem, recv_sem,
):
    dp = lax.axis_index("dp")
    ten = lax.axis_index("tensor")
    core = lax.rem(dp, 2)
    y = lax.rem(dp // 2, 4)
    zl = dp // 8
    x = lax.rem(ten, 4)
    zh = ten // 4

    def to_x(i):
        return (dp, zh * 4 + lax.rem(x + i, 4))

    def to_zh():
        return (dp, (1 - zh) * 4 + x)

    def to_y(i):
        return ((zl * 4 + lax.rem(y + i, 4)) * 2 + core, ten)

    def to_zl(i):
        return ((lax.rem(zl + i, 4) * 4 + y) * 2 + core, ten)

    def to_core():
        return ((zl * 4 + y) * 2 + 1 - core, ten)

    peers = [to_x(1), to_x(2), to_x(3), to_zh(), to_y(1), to_y(2), to_y(3)]
    peers += [to_zl(1), to_zl(2), to_zl(3), to_core()]

    copies = []

    def send(src, dst, device):
        at = len(copies)
        copy = pltpu.make_async_remote_copy(
            src_ref=src,
            dst_ref=dst,
            send_sem=send_sem.at[at],
            recv_sem=recv_sem.at[at],
            device_id=device,
            device_id_type=MESH,
        )
        copy.start()
        copies.append(copy)
        return copy

    def land(batch):
        for copy in batch:
            copy.wait_recv()

    def rows_own(n):
        return pl.ds(pl.multiple_of((core * 16 + y * 4 + zl) * n, n), n)

    def rows_y(n):
        return pl.ds(pl.multiple_of((core * 16 + y * 4) * n, 4 * n), 4 * n)

    def rows_core(n):
        return pl.ds(pl.multiple_of(core * 16 * n, 16 * n), 16 * n)

    def gather_zl(buf, n):
        return [send(buf.at[rows_own(n)], buf.at[rows_own(n)], to_zl(i)) for i in (1, 2, 3)]

    def gather_y(buf, n):
        return [send(buf.at[rows_y(n)], buf.at[rows_y(n)], to_y(i)) for i in (1, 2, 3)]

    def gather_core(buf, n):
        return [send(buf.at[rows_core(n)], buf.at[rows_core(n)], to_core())]

    def gather_start(buf, n):
        own = buf.at[rows_own(n)]
        along_zl = [send(own, own, to_zl(i)) for i in (1, 2, 3)]
        return along_zl, [send(own, own, to_y(i)) for i in (1, 2, 3)]

    def gather_rest(buf, n, started):
        along_zl, along_y = started
        for i, copy in zip((1, 2, 3), along_zl):
            copy.wait_recv()
            at = core * 16 + y * 4 + lax.rem(zl + 4 - i, 4)
            came = buf.at[pl.ds(pl.multiple_of(at * n, n), n)]
            along_y.extend(send(came, came, to_y(k)) for k in (1, 2, 3))
        return along_y

    loads = [
        pltpu.make_async_copy(src, dst, load_sem.at[i])
        for i, (src, dst) in enumerate(
            (
                (refl_hbm, refl_v),
                (tok_hbm, tok_all.at[rows_own(TB)]),
                (gout_hbm, gout_all.at[rows_own(TB)]),
                (gate_hbm, gate_v),
                (up_hbm, up_v),
                (down_hbm, down_v),
            )
        )
    ]
    for load in loads:
        load.start()

    barrier = pltpu.get_barrier_semaphore()
    for peer in peers:
        pl.semaphore_signal(barrier, inc=1, device_id=peer, device_id_type=MESH)

    loads[2].wait()
    pl.semaphore_wait(barrier, len(peers))
    gout_start = gather_start(gout_all, TB)

    loads[0].wait()
    my_half = pl.ds(pl.multiple_of(core * 128, 128), 128)
    columns = jnp.transpose(refl_v[:, my_half])
    gram_v[my_half, :] = jnp.dot(columns, refl_v[...], precision=HI, preferred_element_type=F32)

    def gram_rows(i):
        return pl.ds(pl.multiple_of(core * 128 + lax.rem(x + i, 4) * 32, 32), 32)

    gram_x = [send(gram_v.at[gram_rows(i)], gm_xr.at[i - 1], to_x(i)) for i in (2, 1, 3)]
    gout_y = gather_rest(gout_all, TB, gout_start)
    loads[1].wait()
    own_tok = tok_all[rows_own(TB), :].astype(F32)
    pj_send[...] = jnp.dot(own_tok, refl_v[...], precision=HI, preferred_element_type=F32)
    pj_x = [send(pj_send, pj_xr.at[i - 1], to_x(i)) for i in (2, 1, 3)]
    tok_zl = gather_zl(tok_all, TB)

    land(gram_x)
    gm_zs[...] = gram_v[gram_rows(0), :] + gm_xr[0] + gm_xr[1] + gm_xr[2]
    gram_z = send(gm_zs, gm_zr, to_zh())
    land(pj_x)
    pj_zs[...] = pj_send[...] + pj_xr[0] + pj_xr[1] + pj_xr[2]
    pj_z = send(pj_zs, pj_zr, to_zh())

    land(gout_y)
    gout_core = gather_core(gout_all, TB)
    land(tok_zl)
    tok_y = gather_y(tok_all, TB)
    gram_z.wait_recv()
    gram_all[gram_rows(0), :] = gm_zs[...] + gm_zr[...]
    own_gram = gram_all.at[gram_rows(0)]
    gram_x = [send(own_gram, own_gram, to_x(i)) for i in (2, 1, 3)]
    pj_z.wait_recv()
    pj_all[rows_own(TB), :] = pj_zs[...] + pj_zr[...]
    pj_start = gather_start(pj_all, TB)

    def x_rows(i):
        return pl.ds(pl.multiple_of(lax.rem(x + i, 4) * 128, 128), 128)

    def scatter_x(u, cols, block):
        started = []
        for i in (2, 1, 3):
            p_send[u, x_rows(i), cols] = block(x_rows(i), cols).astype(BF)
            started.append(send(p_send.at[u, x_rows(i), cols], p_xr.at[u, i - 1, :, cols], to_x(i)))
        p_own[u, :, cols] = block(x_rows(0), cols)
        return started

    def exchange_zh(u, cols, started):
        land(started)
        got = p_xr[u, 0, :, cols].astype(F32) + p_xr[u, 1, :, cols].astype(F32)
        total = p_own[u, :, cols] + got + p_xr[u, 2, :, cols].astype(F32)
        p_own[u, :, cols] = total
        p_zs[u, :, cols] = total.astype(BF)
        return send(p_zs.at[u, :, cols], p_zr.at[u, :, cols], to_zh())

    def reduced(u, cols, started):
        started.wait_recv()
        return p_own[u, :, cols] + p_zr[u, :, cols].astype(F32)

    def dh_block(rows, cols):
        return nt(gout_all[rows, :], down_v[cols, :])

    loads[5].wait()
    land(gout_core)
    dh_x = [scatter_x(2, HALVES[0], dh_block)]
    land(gram_x)
    gram_core = send(gram_all.at[my_half], gram_all.at[my_half], to_core())
    dh_x.append(scatter_x(2, HALVES[1], dh_block))
    pj_y = gather_rest(pj_all, TB, pj_start)
    land(tok_y)
    tok_core = gather_core(tok_all, TB)
    gram_core.wait_recv()

    gram = gram_all[...]
    row = lax.broadcasted_iota(jnp.int32, (R, R), 0)
    col = lax.broadcasted_iota(jnp.int32, (R, R), 1)
    eye = row == col
    diag_col = 0.5 * jnp.sum(jnp.where(eye, gram, 0.0), axis=1, keepdims=True)
    diag_row = 0.5 * jnp.sum(jnp.where(eye, gram, 0.0), axis=0, keepdims=True)
    unit_v[...] = jnp.where(col > row, gram, 0.0) / diag_col
    first = (col == row + 1) & ((row & 1) == 0)
    inv_v[...] = jnp.where(eye, 1.0, 0.0) - jnp.where(first, unit_v[...], 0.0)

    def double(level, carry):
        rb = lax.shift_right_logical(row, level)
        cb = lax.shift_right_logical(col, level)
        corner = (cb == rb + 1) & ((rb & 1) == 0)
        m = jnp.where(corner, unit_v[...], 0.0)
        step = jnp.dot(m, inv_v[...], precision=HI, preferred_element_type=F32)
        inv_v[...] -= jnp.dot(inv_v[...], step, precision=HI, preferred_element_type=F32)
        return carry

    lax.fori_loop(1, 4, double, 0)
    land(pj_y)
    pj_core = gather_core(pj_all, TB)
    dh_z = [exchange_zh(2, HALVES[0], dh_x[0])]
    lax.fori_loop(4, 8, double, 0)
    inv_v[...] = inv_v[...] / diag_row
    land(pj_core)
    coef_v[...] = jnp.dot(pj_all[...], inv_v[...], precision=HI, preferred_element_type=F32)
    land(tok_core)
    r_hi, r_lo = split(refl_v[...])
    weights = (gate_v, up_v)
    loads[3].wait()
    loads[4].wait()

    def reflect(rows):
        c_hi, c_lo = split(coef_v[rows, :])
        moved = nt(c_hi, r_hi) + nt(c_lo, r_hi) + nt(c_hi, r_lo)
        reflected[rows, :] = (tok_all[rows, :].astype(F32) - moved).astype(BF)

    def pre_block(u):
        return lambda rows, cols: nn(reflected[rows, :], weights[u][:, cols])

    last = len(COLS) - 1
    pre_x, pre_z, h_x = {}, {}, {}

    def pre_scatter(j):
        for u in range(2):
            pre_x[u, j] = scatter_x(u, COLS[j], pre_block(u))

    def pre_exchange(j):
        for u in range(2):
            pre_z[u, j] = exchange_zh(u, COLS[j], pre_x[u, j])

    def give(u, cols):
        block = h_all.at[u, x_rows(0), cols]
        return [send(block, block, to_x(i)) for i in (2, 1, 3)]

    def half(i, h):
        return pl.ds(pl.multiple_of(lax.rem(x + i, 4) * 128 + h * 64, 64), 64)

    def give_sides(u, cols):
        block = h_all.at[u, x_rows(0), cols]
        return [send(block, block, to_x(i)) for i in (1, 3)]

    def onward(j):
        for u in range(2):
            for i, copy in zip((1, 3), h_x[u, j]):
                copy.wait_recv()
                block = h_all.at[u, half(4 - i, i // 2), COLS[j]]
                h_on.append(send(block, block, to_x(i)))

    h_on = []

    def activate(j):
        cols = COLS[j]
        gate = reduced(0, cols, pre_z[0, j])
        up = reduced(1, cols, pre_z[1, j])
        d_hidden = p_own[2, :, cols] + p_zr[2, :, cols].astype(F32)
        sigma = jax.nn.sigmoid(gate)
        h_all[0, x_rows(0), cols] = (d_hidden * up * sigma * (1.0 + gate * (1.0 - sigma))).astype(BF)
        h_all[1, x_rows(0), cols] = (d_hidden * gate * sigma).astype(BF)
        for u in range(2):
            h_x[u, j] = give(u, cols) if j == last else give_sides(u, cols)
        h_all[2, x_rows(0), cols] = (gate * sigma * up).astype(BF)

    pre_x[0, 0], pre_x[1, 0] = [], []
    for i in (2, 1, 3, 0):
        reflect(x_rows(i))
        for u in range(2):
            value = pre_block(u)(x_rows(i), COLS[0])
            if i:
                p_send[u, x_rows(i), COLS[0]] = value.astype(BF)
                pre_x[u, 0].append(
                    send(p_send.at[u, x_rows(i), COLS[0]], p_xr.at[u, i - 1, :, COLS[0]], to_x(i))
                )
            else:
                p_own[u, :, COLS[0]] = value
    dh_z.append(exchange_zh(2, HALVES[1], dh_x[1]))
    pre_scatter(1)
    pre_exchange(0)
    pre_scatter(2)
    pre_exchange(1)
    pre_scatter(3)

    refl_t[...] = jnp.transpose(refl_v[...])
    t_hi, t_lo = split(refl_t[...])
    for u in range(2):
        rg_hi[u], rg_lo[u] = split(nn(t_hi, weights[u][...]) + nn(t_lo, weights[u][...]))
    coef_t[...] = jnp.transpose(coef_v[...])
    tok_t[...] = jnp.transpose(tok_all[...])
    land(dh_z)
    activate(0)
    pre_exchange(2)
    activate(1)
    pre_exchange(3)
    onward(0)
    activate(2)
    onward(1)
    activate(3)
    onward(2)

    t_hi, t_lo = split(coef_t[...])

    def dc_part(rows, j):
        cols = COLS[j]
        total = jnp.zeros((rows.size, R), F32)
        for u in range(2):
            block = h_all[u, rows, cols]
            total = total + nt(block, rg_hi[u, :, cols]) + nt(block, rg_lo[u, :, cols])
        return total

    def q_part(j):
        cols = COLS[j]
        for u in range(2):
            block = h_all[u, :, cols]
            q_hi[u, :, cols], q_lo[u, :, cols] = split(nn(t_hi, block) + nn(t_lo, block))

    everything = pl.ds(0, TOKENS)
    for j in range(last):
        land(h_on[4 * j : 4 * j + 4])
        dc_acc[...] = dc_part(everything, j) if j == 0 else dc_acc[...] + dc_part(everything, j)
        q_part(j)
    land(h_x[0, last] + h_x[1, last])

    hidden_x = give(2, ALL_COLS)

    half_own = pl.ds(pl.multiple_of(core * 256, 256), 256)
    half_other = pl.ds(pl.multiple_of((1 - core) * 256, 256), 256)

    def dc_block(rows):
        return dc_acc[rows, :] + dc_part(rows, last)

    def scatter_y(own, sent, got, n, dtype):
        started = []
        for i in (2, 1, 3):
            rows = pl.ds(pl.multiple_of(lax.rem(y + i, 4) * 4 * n, 4 * n), 4 * n)
            sent[i - 1] = own[rows, :].astype(dtype)
            started.append(send(sent.at[i - 1], got.at[i - 1], to_y(i)))
        return started

    def after_y(own, got, started, n):
        land(started)
        rows = pl.ds(pl.multiple_of(y * 4 * n, 4 * n), 4 * n)
        own[rows, :] = own[rows, :] + got[0].astype(F32) + got[1].astype(F32) + got[2].astype(F32)

    def scatter_zl(own, sent, got, n, dtype):
        started = []
        for i in (2, 1, 3):
            rows = pl.ds(pl.multiple_of((y * 4 + lax.rem(zl + i, 4)) * n, n), n)
            sent[i - 1] = own[rows, :].astype(dtype)
            started.append(send(sent.at[i - 1], got.at[i - 1], to_zl(i)))
        return started

    def after_zl(own, got, started, n):
        land(started)
        rows = pl.ds(pl.multiple_of((y * 4 + zl) * n, n), n)
        return own[rows, :] + got[0].astype(F32) + got[1].astype(F32) + got[2].astype(F32)

    dc_cs[...] = dc_block(half_other)
    dc_c = send(dc_cs, dc_cr, to_core())
    dc_own[...] = dc_block(half_own)
    dc_c.wait_recv()
    dc_own[...] = dc_own[...] + dc_cr[...]
    dc_y = scatter_y(dc_own, dc_ys, dc_yr, TB, F32)

    q_part(last)

    def g_block(rows):
        total = nt(gate_v[rows, :], q_hi[0]) + nt(gate_v[rows, :], q_lo[0])
        return -(total + nt(up_v[rows, :], q_hi[1]) + nt(up_v[rows, :], q_lo[1]))

    g_half_own = pl.ds(pl.multiple_of(core * 512, 512), 512)
    g_half_other = pl.ds(pl.multiple_of((1 - core) * 512, 512), 512)
    g_cs[...] = g_block(g_half_other).astype(BF)
    g_c = send(g_cs, g_cr, to_core())

    after_y(dc_own, dc_yr, dc_y, TB)
    dc_z = scatter_zl(dc_own, dc_zs, dc_zr, TB, F32)

    g_own[...] = g_block(g_half_own)
    g_c.wait_recv()
    g_own[...] = g_own[...] + g_cr[...].astype(F32)
    g_y = scatter_y(g_own, g_ys, g_yr, DO, BF)

    dc_xs[...] = after_zl(dc_own, dc_zr, dc_z, TB)
    dc_x = [send(dc_xs, dc_xr.at[i - 1], to_x(i)) for i in (1, 2, 3)]

    land(dc_x)
    dc_hs[...] = dc_xs[...] + dc_xr[0] + dc_xr[1] + dc_xr[2]
    dc_h = send(dc_hs, dc_hr, to_zh())

    land(hidden_x)
    mx_cs[...] = nn(h_all[2, half_other, :], down_v[...]).astype(BF)
    mx_c = send(mx_cs, mx_cr, to_core())

    after_y(g_own, g_yr, g_y, DO)
    g_z = scatter_zl(g_own, g_zs, g_zr, DO, BF)

    mx_own[...] = nn(h_all[2, half_own, :], down_v[...])
    mx_c.wait_recv()
    mx_own[...] = mx_own[...] + mx_cr[...].astype(F32)
    mx_y = scatter_y(mx_own, mx_ys, mx_yr, TB, BF)

    dc_h.wait_recv()
    d_coeffs = -(dc_hs[...] + dc_hr[...])
    dp_all[rows_own(TB), :] = lax.dot_general(
        d_coeffs, inv_v[...], (((1,), (1,)), ((), ())), precision=HI, preferred_element_type=F32
    )
    dp_zl = gather_zl(dp_all, TB)

    g_all[rows_own(DO), :] = after_zl(g_own, g_zr, g_z, DO).astype(BF)
    g_zl = gather_zl(g_all, DO)

    land(dp_zl)
    dp_y = gather_y(dp_all, TB)

    after_y(mx_own, mx_yr, mx_y, TB)
    mx_z = scatter_zl(mx_own, mx_zs, mx_zr, TB, BF)

    land(g_zl)
    g_y2 = gather_y(g_all, DO)

    land(dp_y)
    dp_core = gather_core(dp_all, TB)
    mixed_ref[...] = after_zl(mx_own, mx_zr, mx_z, TB).astype(BF)
    land(dp_core)

    d_coupling = -jnp.dot(coef_t[...], dp_all[...], precision=HI, preferred_element_type=F32)
    sym = jnp.where(col >= row, d_coupling, jnp.transpose(d_coupling))
    d_hi, d_lo = split(dp_all[...])
    land(g_y2)
    g_core = gather_core(g_all, DO)
    total = nn(tok_t[...], d_hi) + nn(tok_t[...], d_lo)
    total = total + jnp.dot(refl_v[...], sym, precision=HI, preferred_element_type=F32)
    land(g_core)
    grad_ref[...] = total + g_all[...].astype(F32)

    for copy in copies:
        copy.wait_send()


def scratch():
    v = pltpu.VMEM
    dma = pltpu.SemaphoreType.DMA
    return [
        v((DB, R), F32), v((DB, FB), BF), v((DB, FB), BF), v((FB, DB), BF),
        v((TOKENS, DB), BF), v((TOKENS, DB), BF), v((DB, TOKENS), BF), v((R, DB), F32), v((R, R), F32), v((R, R), F32), v((R, R), F32),
        v((R, R), F32), v((3, 32, R), F32), v((32, R), F32), v((32, R), F32),
        v((TB, R), F32), v((3, TB, R), F32), v((TB, R), F32), v((TB, R), F32), v((TOKENS, R), F32),
        v((2, R, FB), BF), v((2, R, FB), BF), v((TOKENS, DB), BF), v((TOKENS, R), F32), v((R, TOKENS), F32),
        v((3, TOKENS, FB), BF), v((3, 3, 128, FB), BF), v((3, 128, FB), F32), v((3, 128, FB), BF), v((3, 128, FB), BF),
        v((3, TOKENS, FB), BF), v((TOKENS, R), F32), v((2, R, FB), BF), v((2, R, FB), BF),
        v((256, DB), BF), v((256, DB), BF), v((256, DB), F32),
        v((3, 64, DB), BF), v((3, 64, DB), BF), v((3, TB, DB), BF), v((3, TB, DB), BF),
        v((256, R), F32), v((256, R), F32), v((256, R), F32),
        v((3, 64, R), F32), v((3, 64, R), F32), v((3, TB, R), F32), v((3, TB, R), F32),
        v((TB, R), F32), v((3, TB, R), F32), v((TB, R), F32), v((TB, R), F32), v((TOKENS, R), F32),
        v((512, R), BF), v((512, R), BF), v((512, R), F32),
        v((3, 4 * DO, R), BF), v((3, 4 * DO, R), BF), v((3, DO, R), BF), v((3, DO, R), BF), v((DB, R), BF),
        dma((6,)), dma((SEMS,)), dma((SEMS,)),
    ]


def body(tokens, reflectors, gate_weight, up_weight, down_weight, grad_out):
    whole = pl.BlockSpec(memory_space=pltpu.VMEM)
    far = pl.BlockSpec(memory_space=pltpu.HBM)
    return pl.pallas_call(
        kernel,
        out_shape=(
            jax.ShapeDtypeStruct((TB, DB), BF),
            jax.ShapeDtypeStruct((DB, R), F32),
        ),
        in_specs=[far] * 6,
        out_specs=(whole, whole),
        scratch_shapes=scratch(),
        compiler_params=pltpu.CompilerParams(
            collective_id=0, has_side_effects=True, vmem_limit_bytes=52 << 20
        ),
    )(tokens, reflectors, gate_weight, up_weight, down_weight, grad_out)


def solution(mesh):
    placed = (
        P("dp", "tensor"),
        P("tensor", None),
        P("tensor", "dp"),
        P("tensor", "dp"),
        P("dp", "tensor"),
        P("dp", "tensor"),
    )
    return jax.shard_map(
        body,
        mesh=mesh,
        in_specs=placed,
        out_specs=(P("dp", "tensor"), P("tensor", None)),
        check_vma=False,
    )
```

```python
import functools

import jax
import jax.numpy as jnp
from jax import lax
from jax.experimental import pallas as pl
from jax.experimental.pallas import tpu as pltpu
from jax.sharding import PartitionSpec as P

MESH = pl.DeviceIdType.MESH
BF = jnp.bfloat16
F32 = jnp.float32
HI = lax.Precision.HIGHEST

D, FF, R, TOKENS = 8192, 28672, 256, 512
DB = D // 8
FB = FF // 32
TB = TOKENS // 32
DO = DB // 32
SEMS = 224
ALL_COLS = pl.ds(0, FB)
HALVES = (pl.ds(0, 512), pl.ds(512, 384))
COLS = (pl.ds(0, 128), pl.ds(128, 256), pl.ds(384, 256), pl.ds(640, 256))


def nn(a, b):
    return jnp.dot(a, b, preferred_element_type=F32)


def nt(a, b):
    return lax.dot_general(a, b, (((1,), (1,)), ((), ())), preferred_element_type=F32)


def split(v):
    high = v.astype(BF)
    return high, (v - high.astype(F32)).astype(BF)


def kernel(
    tok_hbm, refl_hbm, gate_hbm, up_hbm, down_hbm, gout_hbm, mixed_ref, grad_ref,
    refl_v, gate_v, up_v, down_v, tok_all, gout_all, tok_t, refl_t, gram_v, unit_v, inv_v,
    gram_all, gm_xr, gm_zs, gm_zr, pj_send, pj_xr, pj_zs, pj_zr, pj_all,
    rg_hi, rg_lo, reflected, coef_v, coef_t,
    p_send, p_xr, p_own, p_zs, p_zr,
    h_all, dc_acc, q_hi, q_lo,
    mx_cs, mx_cr, mx_own, mx_ys, mx_yr, mx_zs, mx_zr,
    dc_cs, dc_cr, dc_own, dc_ys, dc_yr, dc_zs, dc_zr, dc_xs, dc_xr, dc_hs, dc_hr, dp_all,
    g_cs, g_cr, g_own, g_ys, g_yr, g_zs, g_zr, g_all,
    load_sem, send_sem, recv_sem,
):
    dp = lax.axis_index("dp")
    ten = lax.axis_index("tensor")
    core = lax.rem(dp, 2)
    y = lax.rem(dp // 2, 4)
    zl = dp // 8
    x = lax.rem(ten, 4)
    zh = ten // 4

    def to_x(i):
        return (dp, zh * 4 + lax.rem(x + i, 4))

    def to_zh():
        return (dp, (1 - zh) * 4 + x)

    def to_y(i):
        return ((zl * 4 + lax.rem(y + i, 4)) * 2 + core, ten)

    def to_zl(i):
        return ((lax.rem(zl + i, 4) * 4 + y) * 2 + core, ten)

    def to_core():
        return ((zl * 4 + y) * 2 + 1 - core, ten)

    peers = [to_x(1), to_x(2), to_x(3), to_zh(), to_y(1), to_y(2), to_y(3)]
    peers += [to_zl(1), to_zl(2), to_zl(3), to_core()]

    copies = []

    def send(src, dst, device):
        at = len(copies)
        copy = pltpu.make_async_remote_copy(
            src_ref=src,
            dst_ref=dst,
            send_sem=send_sem.at[at],
            recv_sem=recv_sem.at[at],
            device_id=device,
            device_id_type=MESH,
        )
        copy.start()
        copies.append(copy)
        return copy

    def land(batch):
        for copy in batch:
            copy.wait_recv()

    def rows_own(n):
        return pl.ds(pl.multiple_of((core * 16 + y * 4 + zl) * n, n), n)

    def rows_y(n):
        return pl.ds(pl.multiple_of((core * 16 + y * 4) * n, 4 * n), 4 * n)

    def rows_core(n):
        return pl.ds(pl.multiple_of(core * 16 * n, 16 * n), 16 * n)

    def gather_zl(buf, n):
        return [send(buf.at[rows_own(n)], buf.at[rows_own(n)], to_zl(i)) for i in (1, 2, 3)]

    def gather_y(buf, n):
        return [send(buf.at[rows_y(n)], buf.at[rows_y(n)], to_y(i)) for i in (1, 2, 3)]

    def gather_core(buf, n):
        return [send(buf.at[rows_core(n)], buf.at[rows_core(n)], to_core())]

    def gather_start(buf, n):
        own = buf.at[rows_own(n)]
        along_zl = [send(own, own, to_zl(i)) for i in (1, 2, 3)]
        return along_zl, [send(own, own, to_y(i)) for i in (1, 2, 3)]

    def gather_rest(buf, n, started):
        along_zl, along_y = started
        for i, copy in zip((1, 2, 3), along_zl):
            copy.wait_recv()
            at = core * 16 + y * 4 + lax.rem(zl + 4 - i, 4)
            came = buf.at[pl.ds(pl.multiple_of(at * n, n), n)]
            along_y.extend(send(came, came, to_y(k)) for k in (1, 2, 3))
        return along_y

    loads = [
        pltpu.make_async_copy(src, dst, load_sem.at[i])
        for i, (src, dst) in enumerate(
            (
                (refl_hbm, refl_v),
                (tok_hbm, tok_all.at[rows_own(TB)]),
                (gout_hbm, gout_all.at[rows_own(TB)]),
                (gate_hbm, gate_v),
                (up_hbm, up_v),
                (down_hbm, down_v),
            )
        )
    ]
    for load in loads:
        load.start()

    barrier = pltpu.get_barrier_semaphore()
    for peer in peers:
        pl.semaphore_signal(barrier, inc=1, device_id=peer, device_id_type=MESH)

    loads[2].wait()
    pl.semaphore_wait(barrier, len(peers))
    gout_start = gather_start(gout_all, TB)

    loads[0].wait()
    my_half = pl.ds(pl.multiple_of(core * 128, 128), 128)
    columns = jnp.transpose(refl_v[:, my_half])
    gram_v[my_half, :] = jnp.dot(columns, refl_v[...], precision=HI, preferred_element_type=F32)

    def gram_rows(i):
        return pl.ds(pl.multiple_of(core * 128 + lax.rem(x + i, 4) * 32, 32), 32)

    gram_x = [send(gram_v.at[gram_rows(i)], gm_xr.at[i - 1], to_x(i)) for i in (2, 1, 3)]
    gout_y = gather_rest(gout_all, TB, gout_start)
    loads[1].wait()
    own_tok = tok_all[rows_own(TB), :].astype(F32)
    pj_send[...] = jnp.dot(own_tok, refl_v[...], precision=HI, preferred_element_type=F32)
    pj_x = [send(pj_send, pj_xr.at[i - 1], to_x(i)) for i in (2, 1, 3)]
    tok_zl = gather_zl(tok_all, TB)

    land(gram_x)
    gm_zs[...] = gram_v[gram_rows(0), :] + gm_xr[0] + gm_xr[1] + gm_xr[2]
    gram_z = send(gm_zs, gm_zr, to_zh())
    land(pj_x)
    pj_zs[...] = pj_send[...] + pj_xr[0] + pj_xr[1] + pj_xr[2]
    pj_z = send(pj_zs, pj_zr, to_zh())

    land(gout_y)
    gout_core = gather_core(gout_all, TB)
    land(tok_zl)
    tok_y = gather_y(tok_all, TB)
    gram_z.wait_recv()
    gram_all[gram_rows(0), :] = gm_zs[...] + gm_zr[...]
    own_gram = gram_all.at[gram_rows(0)]
    gram_x = [send(own_gram, own_gram, to_x(i)) for i in (2, 1, 3)]
    pj_z.wait_recv()
    pj_all[rows_own(TB), :] = pj_zs[...] + pj_zr[...]
    pj_start = gather_start(pj_all, TB)

    def x_rows(i):
        return pl.ds(pl.multiple_of(lax.rem(x + i, 4) * 128, 128), 128)

    def scatter_x(u, cols, block):
        started = []
        for i in (2, 1, 3):
            p_send[u, x_rows(i), cols] = block(x_rows(i), cols).astype(BF)
            started.append(send(p_send.at[u, x_rows(i), cols], p_xr.at[u, i - 1, :, cols], to_x(i)))
        p_own[u, :, cols] = block(x_rows(0), cols)
        return started

    def exchange_zh(u, cols, started):
        land(started)
        got = p_xr[u, 0, :, cols].astype(F32) + p_xr[u, 1, :, cols].astype(F32)
        total = p_own[u, :, cols] + got + p_xr[u, 2, :, cols].astype(F32)
        p_own[u, :, cols] = total
        p_zs[u, :, cols] = total.astype(BF)
        return send(p_zs.at[u, :, cols], p_zr.at[u, :, cols], to_zh())

    def reduced(u, cols, started):
        started.wait_recv()
        return p_own[u, :, cols] + p_zr[u, :, cols].astype(F32)

    def dh_block(rows, cols):
        return nt(gout_all[rows, :], down_v[cols, :])

    loads[5].wait()
    land(gout_core)
    dh_x = [scatter_x(2, HALVES[0], dh_block)]
    land(gram_x)
    gram_core = send(gram_all.at[my_half], gram_all.at[my_half], to_core())
    dh_x.append(scatter_x(2, HALVES[1], dh_block))
    pj_y = gather_rest(pj_all, TB, pj_start)
    land(tok_y)
    tok_core = gather_core(tok_all, TB)
    gram_core.wait_recv()

    gram = gram_all[...]
    row = lax.broadcasted_iota(jnp.int32, (R, R), 0)
    col = lax.broadcasted_iota(jnp.int32, (R, R), 1)
    eye = row == col
    diag_col = 0.5 * jnp.sum(jnp.where(eye, gram, 0.0), axis=1, keepdims=True)
    diag_row = 0.5 * jnp.sum(jnp.where(eye, gram, 0.0), axis=0, keepdims=True)
    unit_v[...] = jnp.where(col > row, gram, 0.0) / diag_col
    first = (col == row + 1) & ((row & 1) == 0)
    inv_v[...] = jnp.where(eye, 1.0, 0.0) - jnp.where(first, unit_v[...], 0.0)

    def double(level, carry):
        rb = lax.shift_right_logical(row, level)
        cb = lax.shift_right_logical(col, level)
        corner = (cb == rb + 1) & ((rb & 1) == 0)
        m = jnp.where(corner, unit_v[...], 0.0)
        step = jnp.dot(m, inv_v[...], precision=HI, preferred_element_type=F32)
        inv_v[...] -= jnp.dot(inv_v[...], step, precision=HI, preferred_element_type=F32)
        return carry

    lax.fori_loop(1, 4, double, 0)
    land(pj_y)
    pj_core = gather_core(pj_all, TB)
    dh_z = [exchange_zh(2, HALVES[0], dh_x[0])]
    lax.fori_loop(4, 8, double, 0)
    inv_v[...] = inv_v[...] / diag_row
    dh_z.append(exchange_zh(2, HALVES[1], dh_x[1]))
    land(pj_core)
    coef_v[...] = jnp.dot(pj_all[...], inv_v[...], precision=HI, preferred_element_type=F32)
    land(tok_core)
    r_hi, r_lo = split(refl_v[...])
    weights = (gate_v, up_v)
    loads[3].wait()
    loads[4].wait()

    def reflect(rows):
        c_hi, c_lo = split(coef_v[rows, :])
        moved = nt(c_hi, r_hi) + nt(c_lo, r_hi) + nt(c_hi, r_lo)
        reflected[rows, :] = (tok_all[rows, :].astype(F32) - moved).astype(BF)

    def pre_block(u):
        return lambda rows, cols: nn(reflected[rows, :], weights[u][:, cols])

    last = len(COLS) - 1
    pre_x, pre_z, h_x = {}, {}, {}

    def pre_scatter(j):
        for u in range(2):
            pre_x[u, j] = scatter_x(u, COLS[j], pre_block(u))

    def pre_exchange(j):
        for u in range(2):
            pre_z[u, j] = exchange_zh(u, COLS[j], pre_x[u, j])

    def give(u, cols):
        block = h_all.at[u, x_rows(0), cols]
        return [send(block, block, to_x(i)) for i in (2, 1, 3)]

    def half(i, h):
        return pl.ds(pl.multiple_of(lax.rem(x + i, 4) * 128 + h * 64, 64), 64)

    def give_sides(u, cols):
        block = h_all.at[u, x_rows(0), cols]
        return [send(block, block, to_x(i)) for i in (1, 3)]

    def onward(j):
        for u in range(2):
            for i, copy in zip((1, 3), h_x[u, j]):
                copy.wait_recv()
                block = h_all.at[u, half(4 - i, i // 2), COLS[j]]
                h_on.append(send(block, block, to_x(i)))

    h_on = []

    def activate(j):
        cols = COLS[j]
        gate = reduced(0, cols, pre_z[0, j])
        up = reduced(1, cols, pre_z[1, j])
        d_hidden = p_own[2, :, cols] + p_zr[2, :, cols].astype(F32)
        sigma = jax.nn.sigmoid(gate)
        h_all[0, x_rows(0), cols] = (d_hidden * up * sigma * (1.0 + gate * (1.0 - sigma))).astype(BF)
        h_all[1, x_rows(0), cols] = (d_hidden * gate * sigma).astype(BF)
        for u in range(2):
            h_x[u, j] = give(u, cols) if j == last else give_sides(u, cols)
        h_all[2, x_rows(0), cols] = (gate * sigma * up).astype(BF)

    pre_x[0, 0], pre_x[1, 0] = [], []
    for i in (2, 1, 3, 0):
        reflect(x_rows(i))
        for u in range(2):
            value = pre_block(u)(x_rows(i), COLS[0])
            if i:
                p_send[u, x_rows(i), COLS[0]] = value.astype(BF)
                pre_x[u, 0].append(
                    send(p_send.at[u, x_rows(i), COLS[0]], p_xr.at[u, i - 1, :, COLS[0]], to_x(i))
                )
            else:
                p_own[u, :, COLS[0]] = value
    pre_scatter(1)
    pre_exchange(0)
    pre_scatter(2)
    pre_exchange(1)
    pre_scatter(3)

    refl_t[...] = jnp.transpose(refl_v[...])
    t_hi, t_lo = split(refl_t[...])
    for u in range(2):
        rg_hi[u], rg_lo[u] = split(nn(t_hi, weights[u][...]) + nn(t_lo, weights[u][...]))
    coef_t[...] = jnp.transpose(coef_v[...])
    tok_t[...] = jnp.transpose(tok_all[...])
    land(dh_z)
    activate(0)
    pre_exchange(2)
    activate(1)
    pre_exchange(3)
    onward(0)
    activate(2)
    onward(1)
    activate(3)
    onward(2)

    t_hi, t_lo = split(coef_t[...])

    def dc_part(rows, j):
        cols = COLS[j]
        total = jnp.zeros((rows.size, R), F32)
        for u in range(2):
            block = h_all[u, rows, cols]
            total = total + nt(block, rg_hi[u, :, cols]) + nt(block, rg_lo[u, :, cols])
        return total

    def q_part(j):
        cols = COLS[j]
        for u in range(2):
            block = h_all[u, :, cols]
            q_hi[u, :, cols], q_lo[u, :, cols] = split(nn(t_hi, block) + nn(t_lo, block))

    everything = pl.ds(0, TOKENS)
    for j in range(last):
        land(h_on[4 * j : 4 * j + 4])
        dc_acc[...] = dc_part(everything, j) if j == 0 else dc_acc[...] + dc_part(everything, j)
        q_part(j)
    land(h_x[0, last] + h_x[1, last])

    hidden_x = give(2, ALL_COLS)

    half_own = pl.ds(pl.multiple_of(core * 256, 256), 256)
    half_other = pl.ds(pl.multiple_of((1 - core) * 256, 256), 256)

    def dc_block(rows):
        return dc_acc[rows, :] + dc_part(rows, last)

    def scatter_y(own, sent, got, n, dtype):
        started = []
        for i in (2, 1, 3):
            rows = pl.ds(pl.multiple_of(lax.rem(y + i, 4) * 4 * n, 4 * n), 4 * n)
            sent[i - 1] = own[rows, :].astype(dtype)
            started.append(send(sent.at[i - 1], got.at[i - 1], to_y(i)))
        return started

    def after_y(own, got, started, n):
        land(started)
        rows = pl.ds(pl.multiple_of(y * 4 * n, 4 * n), 4 * n)
        own[rows, :] = own[rows, :] + got[0].astype(F32) + got[1].astype(F32) + got[2].astype(F32)

    def scatter_zl(own, sent, got, n, dtype):
        started = []
        for i in (2, 1, 3):
            rows = pl.ds(pl.multiple_of((y * 4 + lax.rem(zl + i, 4)) * n, n), n)
            sent[i - 1] = own[rows, :].astype(dtype)
            started.append(send(sent.at[i - 1], got.at[i - 1], to_zl(i)))
        return started

    def after_zl(own, got, started, n):
        land(started)
        rows = pl.ds(pl.multiple_of((y * 4 + zl) * n, n), n)
        return own[rows, :] + got[0].astype(F32) + got[1].astype(F32) + got[2].astype(F32)

    dc_cs[...] = dc_block(half_other).astype(BF)
    dc_c = send(dc_cs, dc_cr, to_core())
    dc_own[...] = dc_block(half_own)
    dc_c.wait_recv()
    dc_own[...] = dc_own[...] + dc_cr[...].astype(F32)
    dc_y = scatter_y(dc_own, dc_ys, dc_yr, TB, BF)

    q_part(last)

    def g_block(rows):
        total = nt(gate_v[rows, :], q_hi[0]) + nt(gate_v[rows, :], q_lo[0])
        return -(total + nt(up_v[rows, :], q_hi[1]) + nt(up_v[rows, :], q_lo[1]))

    g_half_own = pl.ds(pl.multiple_of(core * 512, 512), 512)
    g_half_other = pl.ds(pl.multiple_of((1 - core) * 512, 512), 512)
    g_cs[...] = g_block(g_half_other).astype(BF)
    g_c = send(g_cs, g_cr, to_core())

    after_y(dc_own, dc_yr, dc_y, TB)
    dc_z = scatter_zl(dc_own, dc_zs, dc_zr, TB, BF)

    g_own[...] = g_block(g_half_own)
    g_c.wait_recv()
    g_own[...] = g_own[...] + g_cr[...].astype(F32)
    g_y = scatter_y(g_own, g_ys, g_yr, DO, BF)

    dc_xs[...] = after_zl(dc_own, dc_zr, dc_z, TB)
    dc_x = [send(dc_xs, dc_xr.at[i - 1], to_x(i)) for i in (1, 2, 3)]

    land(dc_x)
    dc_hs[...] = dc_xs[...] + dc_xr[0] + dc_xr[1] + dc_xr[2]
    dc_h = send(dc_hs, dc_hr, to_zh())

    land(hidden_x)
    mx_cs[...] = nn(h_all[2, half_other, :], down_v[...]).astype(BF)
    mx_c = send(mx_cs, mx_cr, to_core())

    after_y(g_own, g_yr, g_y, DO)
    g_z = scatter_zl(g_own, g_zs, g_zr, DO, BF)

    mx_own[...] = nn(h_all[2, half_own, :], down_v[...])
    mx_c.wait_recv()
    mx_own[...] = mx_own[...] + mx_cr[...].astype(F32)
    mx_y = scatter_y(mx_own, mx_ys, mx_yr, TB, BF)

    dc_h.wait_recv()
    d_coeffs = -(dc_hs[...] + dc_hr[...])
    d_proj = lax.dot_general(
        d_coeffs, inv_v[...], (((1,), (1,)), ((), ())), precision=HI, preferred_element_type=F32
    )
    dp_all[rows_own(TB), :] = d_proj.astype(BF)
    dp_zl = gather_zl(dp_all, TB)

    g_all[rows_own(DO), :] = after_zl(g_own, g_zr, g_z, DO).astype(BF)
    g_zl = gather_zl(g_all, DO)

    land(dp_zl)
    dp_y = gather_y(dp_all, TB)

    after_y(mx_own, mx_yr, mx_y, TB)
    mx_z = scatter_zl(mx_own, mx_zs, mx_zr, TB, BF)

    land(g_zl)
    g_y2 = gather_y(g_all, DO)

    land(dp_y)
    dp_core = gather_core(dp_all, TB)
    mixed_ref[...] = after_zl(mx_own, mx_zr, mx_z, TB).astype(BF)
    land(dp_core)

    c_hi, c_lo = split(coef_t[...])
    d_coupling = -(nn(c_hi, dp_all[...]) + nn(c_lo, dp_all[...]))
    sym = jnp.where(col >= row, d_coupling, jnp.transpose(d_coupling))
    land(g_y2)
    g_core = gather_core(g_all, DO)
    total = nn(tok_t[...], dp_all[...])
    total = total + jnp.dot(refl_v[...], sym, precision=HI, preferred_element_type=F32)
    land(g_core)
    grad_ref[...] = total + g_all[...].astype(F32)

    for copy in copies:
        copy.wait_send()


def scratch():
    v = pltpu.VMEM
    dma = pltpu.SemaphoreType.DMA
    return [
        v((DB, R), F32), v((DB, FB), BF), v((DB, FB), BF), v((FB, DB), BF),
        v((TOKENS, DB), BF), v((TOKENS, DB), BF), v((DB, TOKENS), BF), v((R, DB), F32), v((R, R), F32), v((R, R), F32), v((R, R), F32),
        v((R, R), F32), v((3, 32, R), F32), v((32, R), F32), v((32, R), F32),
        v((TB, R), F32), v((3, TB, R), F32), v((TB, R), F32), v((TB, R), F32), v((TOKENS, R), F32),
        v((2, R, FB), BF), v((2, R, FB), BF), v((TOKENS, DB), BF), v((TOKENS, R), F32), v((R, TOKENS), F32),
        v((3, TOKENS, FB), BF), v((3, 3, 128, FB), BF), v((3, 128, FB), F32), v((3, 128, FB), BF), v((3, 128, FB), BF),
        v((3, TOKENS, FB), BF), v((TOKENS, R), F32), v((2, R, FB), BF), v((2, R, FB), BF),
        v((256, DB), BF), v((256, DB), BF), v((256, DB), F32),
        v((3, 64, DB), BF), v((3, 64, DB), BF), v((3, TB, DB), BF), v((3, TB, DB), BF),
        v((256, R), BF), v((256, R), BF), v((256, R), F32),
        v((3, 64, R), BF), v((3, 64, R), BF), v((3, TB, R), BF), v((3, TB, R), BF),
        v((TB, R), F32), v((3, TB, R), F32), v((TB, R), F32), v((TB, R), F32), v((TOKENS, R), BF),
        v((512, R), BF), v((512, R), BF), v((512, R), F32),
        v((3, 4 * DO, R), BF), v((3, 4 * DO, R), BF), v((3, DO, R), BF), v((3, DO, R), BF), v((DB, R), BF),
        dma((6,)), dma((SEMS,)), dma((SEMS,)),
    ]


def body(tokens, reflectors, gate_weight, up_weight, down_weight, grad_out):
    whole = pl.BlockSpec(memory_space=pltpu.VMEM)
    far = pl.BlockSpec(memory_space=pltpu.HBM)
    return pl.pallas_call(
        kernel,
        out_shape=(
            jax.ShapeDtypeStruct((TB, DB), BF),
            jax.ShapeDtypeStruct((DB, R), F32),
        ),
        in_specs=[far] * 6,
        out_specs=(whole, whole),
        scratch_shapes=scratch(),
        compiler_params=pltpu.CompilerParams(
            collective_id=0, has_side_effects=True, vmem_limit_bytes=52 << 20
        ),
    )(tokens, reflectors, gate_weight, up_weight, down_weight, grad_out)


def solution(mesh):
    placed = (
        P("dp", "tensor"),
        P("tensor", None),
        P("tensor", "dp"),
        P("tensor", "dp"),
        P("dp", "tensor"),
        P("dp", "tensor"),
    )
    return jax.shard_map(
        body,
        mesh=mesh,
        in_specs=placed,
        out_specs=(P("dp", "tensor"), P("tensor", None)),
        check_vma=False,
    )
```
